32 devices in a mesh: groups: 2 (over x), pool: 4 (over y, core), tensor: 4 (over z).
Axes of the slice: x: 2, y: 2, z: 4, core: 2. Of those that a mesh axis runs over, the one named last changes fastest.
Arguments:
- hidden: bfloat16 [1024, 28672], P(('groups', 'pool'), 'tensor'), parts along dimension 0, may hold values from -6 to 6
- down_matrix: bfloat16 [28672, 8192], P('tensor', 'pool'), may hold values from -0.03125 to 0.03125
- adapter_shrink_weight: bfloat16 [16, 16, 28672], P('pool', None, 'tensor'), may hold values from -0.03125 to 0.03125
- adapter_expand_weight: bfloat16 [16, 16, 8192], P(None, None, 'pool'), may hold values from -1.5 to 1.5
- segment_adapter_id: int32 [64], P('groups'), parts along dimension 0, may hold values from 0 to 15
- adapter_storage_slot: int32 [16], replicated, may hold values from 0 to 15, each once
- segment_row_count: int32 [64], P('groups'), parts along dimension 0, may hold values from 1 to 16
Outputs:
- projected: bfloat16 [1024, 8192], P(('groups', 'tensor'), 'pool'), parts along dimension 0
The draws below stay inside these ranges and needn't reach their ends.
There are 2 independent parts, one for each index of `groups`. The reference program is written for one: setup_inputs(seed, part) draws one part's arguments, and reference() takes and returns one part's arrays. A program takes and returns all parts, laid end to end along the dimension named above; an argument that names none is the same for every part. Nothing has to cross between parts.
All inputs are finite; a program needn't handle non-finite values.
Results may differ from the reference program's by a relative error of at most 0.001.
Values may be sent and summed in bfloat16 or wider, within the bound.
A program may use at most 128 MiB of HBM per device.

```python
import math
import jax
import jax.numpy as jnp
import numpy as np
from jax import lax

MODEL_WIDTH = 8192
HIDDEN_UNITS = 28672
ADAPTER_RANK = 16
SEGMENT_ROWS = 16
SEGS = 32
ROWS = 512
ADAPTER_POOL = 16


def touch_ends(array, stream_key, smallest, largest):
    extent = array.shape
    spot = [jax.random.randint(jax.random.fold_in(stream_key, axis), (), 0, extent[axis]) for axis in range(len(extent))]
    array = array.at[tuple(spot)].set(smallest)
    longest = extent.index(max(extent))
    spot[longest] = (spot[longest] + 1) % extent[longest]
    return array.at[tuple(spot)].set(largest)


def block_levels(key, dims, cuts, smallest, high):
    factor_of, own = 1.0, jax.random.fold_in(key, 6)
    for axis_at, parts in cuts:
        heights = jnp.exp(jax.random.uniform(jax.random.fold_in(own, axis_at), (parts,), jnp.float32, smallest / len(cuts), high / len(cuts)))
        factor_of = factor_of * jnp.repeat(heights, dims[axis_at] // parts).reshape([-1 if axis == axis_at else 1 for axis in range(len(dims))])
    return factor_of


def cumulative_ranks(number_of, slope):
    weights = [(1 << 20) // math.isqrt(rank ** slope) + 1 for rank in range(1, number_of + 1)]
    deviation = 1 + sum(weights) // (1 << 30)
    return np.cumsum(np.array([max(1, weight // deviation) for weight in weights]))


def skewed_ids(rng, extent, count, skew):
    table = cumulative_ranks(count, skew)
    pick = jax.random.randint(jax.random.fold_in(rng, 1), extent, 0, int(table[count - 1]))
    rank = jnp.searchsorted(jnp.asarray(table, jnp.int32), pick, side="right")
    return jax.random.permutation(jax.random.fold_in(rng, 2), count)[rank].astype(jnp.int32)


def scatter_about(own_key, dims, spread, most, split=(), kind=jnp.bfloat16):
    result = spread * jax.random.normal(own_key, dims, jnp.float32)
    if split:
        result = result * block_levels(own_key, dims, split, -0.22, 0.18)
    return jnp.clip(result, -most, most).astype(kind)


def setup_inputs(seed: int = 0, part: int = 0) -> dict:
    key_of = jax.random.split(jax.random.key(seed), 8)
    part_splits = jax.random.split(jax.random.fold_in(key_of[7], part), 8)
    return {
        "hidden": scatter_about(part_splits[0], (ROWS, HIDDEN_UNITS), 1.0, 6.0, ((0, 4), (1, 4))),
        "down_matrix": scatter_about(key_of[1], (HIDDEN_UNITS, MODEL_WIDTH), HIDDEN_UNITS ** -0.5, 0.03125, ((0, 4), (1, 4))),
        "adapter_shrink_weight": scatter_about(key_of[2], (ADAPTER_POOL, ADAPTER_RANK, HIDDEN_UNITS), HIDDEN_UNITS ** -0.5, 0.03125, ((0, 4), (2, 4))),
        "adapter_expand_weight": scatter_about(key_of[3], (ADAPTER_POOL, ADAPTER_RANK, MODEL_WIDTH), ADAPTER_RANK ** -0.5, 1.5, ((2, 4),)),
        "segment_adapter_id": touch_ends(skewed_ids(part_splits[4], (SEGS,), ADAPTER_POOL, 2), jax.random.fold_in(part_splits[4], 3), 0, ADAPTER_POOL - 1).astype(jnp.int32),
        "adapter_storage_slot": jax.random.permutation(key_of[5], ADAPTER_POOL).astype(jnp.int32),
        "segment_row_count": touch_ends(jax.random.randint(part_splits[6], (SEGS,), 1, SEGMENT_ROWS + 1), jax.random.fold_in(part_splits[6], 1), 1, SEGMENT_ROWS).astype(jnp.int32),
    }


adapter_scale = 2.0


def reference(hidden, down_matrix, adapter_shrink_weight, adapter_expand_weight, segment_adapter_id, adapter_storage_slot, segment_row_count):
    base_output = jnp.dot(hidden, down_matrix, preferred_element_type=jnp.float32)
    storage_slot_index = jnp.take(adapter_storage_slot, segment_adapter_id, axis=0).astype(jnp.int32)
    selected_shrink = jnp.take(adapter_shrink_weight, storage_slot_index, axis=0).astype(jnp.float32)
    h_seg = hidden.reshape(SEGS, SEGMENT_ROWS, HIDDEN_UNITS).astype(jnp.float32)
    shrink = jnp.einsum("sgf,sqf->sgq", h_seg, selected_shrink, precision=lax.Precision.HIGHEST)
    selected_expand = jnp.take(adapter_expand_weight, storage_slot_index, axis=0).astype(jnp.float32)
    expand_output = jnp.einsum("sgq,sqd->sgd", shrink, selected_expand, precision=lax.Precision.HIGHEST).reshape(ROWS, MODEL_WIDTH)
    valid_mask = (jnp.arange(SEGMENT_ROWS, dtype=jnp.int32)[None, :] < segment_row_count[:, None]).reshape(ROWS)
    return jnp.where(valid_mask[:, None], base_output + adapter_scale * expand_output, 0.0).astype(jnp.bfloat16)
```

```python
import jax
import jax.numpy as jnp
from jax import lax
from jax.experimental import pallas as pl
from jax.experimental.pallas import tpu as pltpu
from jax.sharding import PartitionSpec as P

SEGMENT_ROWS = 16


adapter_scale = 2.0


def per_device(
    hidden,
    down_matrix,
    adapter_shrink_weight,
    adapter_expand_weight,
    segment_adapter_id,
    adapter_storage_slot,
    segment_row_count,
):
    gathered = lax.all_gather(hidden, "pool", axis=0, tiled=True)
    total_rows, ff_local = gathered.shape
    segments = total_rows // SEGMENT_ROWS
    base_output = jnp.dot(gathered, down_matrix, preferred_element_type=jnp.float32)
    adapter_ids = adapter_expand_weight.shape[0]
    same_id = segment_adapter_id[:, None] == jnp.arange(adapter_ids, dtype=jnp.int32)[None, :]
    storage_slot_index = jnp.sum(jnp.where(same_id, adapter_storage_slot[None, :], 0), axis=1)
    h_seg = gathered.reshape(segments, SEGMENT_ROWS, ff_local)
    every_adapter_id = lax.all_gather(adapter_shrink_weight, "pool", axis=0, tiled=True)
    chosen = jnp.take(every_adapter_id, storage_slot_index, axis=0)
    shrink = jnp.einsum("sgf,sqf->sgq", h_seg, chosen, preferred_element_type=jnp.float32)
    local_row_block = lax.psum_scatter(base_output, "tensor", scatter_dimension=0, tiled=True)
    local_segment_list = segments // lax.axis_size("tensor")
    first_seg = lax.axis_index("tensor") * local_segment_list
    whole_shrink = lax.psum(shrink, "tensor")
    own_shrink = lax.dynamic_slice_in_dim(whole_shrink, first_seg, local_segment_list, 0)
    owned_storage_slots = lax.dynamic_slice_in_dim(
        storage_slot_index, first_seg, local_segment_list, 0
    )
    owned_expand_weight = jnp.take(adapter_expand_weight, owned_storage_slots, axis=0).astype(
        jnp.float32
    )
    expand_output = jnp.einsum(
        "sgq,sqd->sgd", own_shrink, owned_expand_weight, precision=lax.Precision.HIGHEST
    )
    local_row_block = local_row_block + adapter_scale * expand_output.reshape(
        local_segment_list * SEGMENT_ROWS, -1
    )
    counts = lax.dynamic_slice_in_dim(segment_row_count, first_seg, local_segment_list, 0)
    valid_mask = (jnp.arange(SEGMENT_ROWS, dtype=jnp.int32)[None, :] < counts[:, None]).reshape(-1)
    return jnp.where(valid_mask[:, None], local_row_block, 0.0).astype(jnp.bfloat16)


MESH = pl.DeviceIdType.MESH
LEVELS = 32500.0
TILES = 4
VMEM_LIMIT = 60 * 2**20
CHUNKS = 4


def fused_kernel(
    id_ref, slot_ref, count_ref, hidden_ref, down_ref, shrink_ref, expand_ref, out_ref,
    h, w, a, e, acc, q_send, q_recv, s_send, s_recv, r_send, r_recv,
    w_sem, load_sem, y_send_sem, y_recv_sem, c_send_sem, c_recv_sem, f_send_sem, f_recv_sem,
    q_send_sem, q_recv_sem, s_send_sem, s_recv_sem, r_send_sem, r_recv_sem,
):
    pools, steps = lax.axis_size("pool"), lax.axis_size("tensor")
    g, p, z = lax.axis_index("groups"), lax.axis_index("pool"), lax.axis_index("tensor")
    y, c = p // 2, p % 2
    core_peer = y * 2 + (1 - c)
    y_peer = (1 - y) * 2 + c
    block, ff = h.shape[1], h.shape[2]
    tile = w.shape[2]
    part = block // CHUNKS
    rank = r_send.shape[1]
    owned = a.shape[0] // rank

    def remote(src, dst, send, recv, pool, step):
        return pltpu.make_async_remote_copy(
            src_ref=src, dst_ref=dst, send_sem=send, recv_sem=recv,
            device_id=(g, pool, step), device_id_type=MESH,
        )

    def w_copy(n):
        return pltpu.make_async_copy(
            down_ref.at[:, pl.ds(pl.multiple_of(n * tile, tile), tile)], w.at[n], w_sem.at[n]
        )

    own_load = pltpu.make_async_copy(hidden_ref, h.at[p], load_sem.at[0])
    a_load = pltpu.make_async_copy(shrink_ref, a, load_sem.at[1])
    e_load = pltpu.make_async_copy(expand_ref, e, load_sem.at[2])
    own_load.start()
    for n in range(TILES):
        w_copy(n).start()

    barrier = pltpu.get_barrier_semaphore()
    for i in range(1, pools * steps):
        other = (p * steps + z + i) % (pools * steps)
        pl.semaphore_signal(
            barrier, inc=1, device_id=(g, other // steps, other % steps), device_id_type=MESH
        )
    pl.semaphore_wait(barrier, pools * steps - 1)

    def y_copy(k, blk):
        rows = pl.ds(pl.multiple_of(k * part, part), part)
        return remote(
            hidden_ref.at[rows], h.at[blk, rows], y_send_sem.at[k], y_recv_sem.at[k], y_peer, z
        )

    def fwd_copy(k, blk):
        rows = pl.ds(pl.multiple_of(k * part, part), part)
        return remote(
            h.at[blk, rows], h.at[blk, rows], f_send_sem.at[k], f_recv_sem.at[k], core_peer, z
        )

    def core_copy(blk):
        return remote(hidden_ref, h.at[blk], c_send_sem.at[0], c_recv_sem.at[0], core_peer, z)

    y_copy(0, p).start()
    core_copy(p).start()
    for k in range(1, CHUNKS):
        y_copy(k, p).start()
    a_load.start()
    e_load.start()

    def emit(x, n, blk, first, rows, scales):
        top = jnp.max(jnp.abs(x), axis=1, keepdims=True)
        scale = (jnp.maximum(top, 1e-30) * (1.0 / LEVELS)).astype(jnp.bfloat16).astype(jnp.float32)
        coded = jnp.round(x * (1.0 / scale)).astype(jnp.int32).astype(jnp.int16)
        cols = pl.ds(pl.multiple_of(n * tile, tile), tile)
        here = pl.ds(pl.multiple_of(first, 16), rows)

        @pl.when(blk == z)
        def _():
            acc[here, cols] = x

        @pl.when(blk != z)
        def _():
            q_send[blk, here, cols] = coded
            remote(
                q_send.at[blk, here, cols], q_recv.at[z, here, cols],
                q_send_sem.at[blk], q_recv_sem.at[z], p, blk,
            ).start()

        lane = lax.broadcasted_iota(jnp.int32, scales.shape, 1)
        return jnp.where(lane == n, scale, scales)

    def emit_scales(scales, blk, first, rows):
        here = pl.ds(pl.multiple_of(first, 16), rows)

        @pl.when(blk != z)
        def _():
            s_send[blk, here] = scales.astype(jnp.bfloat16)
            remote(
                s_send.at[blk, here], s_recv.at[z, here],
                s_send_sem.at[blk], s_recv_sem.at[z], p, blk,
            ).start()

    def slots_of(blk):
        per = block // SEGMENT_ROWS
        lane = lax.broadcasted_iota(jnp.int32, (1, block), 1)
        vec = jnp.zeros((1, block), jnp.int32)
        for i in range(per):
            vec = jnp.where(lane >= i * SEGMENT_ROWS, slot_ref[id_ref[blk * per + i]], vec)
        return vec

    def shrink_block(blk):
        s = lax.dot_general(
            a[...], h[blk], (((1,), (1,)), ((), ())), preferred_element_type=jnp.float32
        )
        row_slot = lax.broadcasted_iota(jnp.int32, s.shape, 0) // rank + owned * p
        s = jnp.where(row_slot == slots_of(blk), s, 0.0)
        total = s[0:rank]
        for i in range(1, owned):
            total = total + s[i * rank:(i + 1) * rank]
        r_send[blk] = total
        me = p * steps + z

        @pl.when(blk == z)
        def _():
            r_recv[me] = total

        for i in range(pools):
            @pl.when(jnp.logical_or(blk != z, p != i))
            def _():
                remote(
                    r_send.at[blk], r_recv.at[me],
                    r_send_sem.at[blk * pools + i], r_recv_sem.at[me], i, blk,
                ).start()

    own_load.wait()
    remote(
        hidden_ref, h.at[core_peer], c_send_sem.at[0], c_recv_sem.at[0], core_peer, z
    ).wait_recv()

    def near(n, scales):
        w_copy(n).wait()
        lhs = jnp.concatenate([h[y * 2], h[y * 2 + 1]], axis=0)
        x = jnp.dot(lhs, w[n], preferred_element_type=jnp.float32)
        return tuple(
            emit(x[j * block:(j + 1) * block], n, y * 2 + j, 0, block, scales[j]) for j in range(2)
        )

    zero = jnp.zeros((block, 128), jnp.float32)
    scales = lax.fori_loop(0, TILES, near, (zero, zero))
    for j in range(2):
        emit_scales(scales[j], y * 2 + j, 0, block)

    a_load.wait()

    def near_shrink(j, _):
        shrink_block(y * 2 + j)
        return 0

    lax.fori_loop(0, 2, near_shrink, 0)

    def far(k, _):
        y_copy(k, y_peer).wait_recv()
        fwd_copy(k, y_peer).start()
        far_first = (1 - y) * 2
        fwd_copy(k, far_first + (1 - c)).wait_recv()
        first = pl.multiple_of(k * part, part)
        rows = pl.ds(first, part)

        def body(n, scales):
            lhs = jnp.concatenate([h[far_first, rows], h[far_first + 1, rows]], axis=0)
            x = jnp.dot(lhs, w[n], preferred_element_type=jnp.float32)
            return tuple(
                emit(x[j * part:(j + 1) * part], n, far_first + j, first, part, scales[j])
                for j in range(2)
            )

        zero = jnp.zeros((part, 128), jnp.float32)
        scales = lax.fori_loop(0, TILES, body, (zero, zero))
        for j in range(2):
            emit_scales(scales[j], far_first + j, first, part)
        return 0

    lax.fori_loop(0, CHUNKS, far, 0)

    def far_shrink(j, _):
        shrink_block((1 - y) * 2 + j)
        return 0

    lax.fori_loop(0, 2, far_shrink, 0)

    me = p * steps + z
    e_load.wait()
    for i in range(pools * steps):
        @pl.when(me != i)
        def _():
            remote(
                r_recv.at[i], r_recv.at[i], r_send_sem.at[i], r_recv_sem.at[i], p, z
            ).wait_recv()
    whole = r_recv[0]
    for i in range(1, pools * steps):
        whole = whole + r_recv[i]
    adapters = e.shape[0] // rank
    spread = jnp.concatenate([whole] * adapters, axis=0)
    row_slot = lax.broadcasted_iota(jnp.int32, spread.shape, 0) // rank
    spread = jnp.where(row_slot == slots_of(z), spread, 0.0).T
    hi = spread.astype(jnp.bfloat16)
    rest = spread - hi.astype(jnp.float32)
    mid = rest.astype(jnp.bfloat16)
    low = (rest - mid.astype(jnp.float32)).astype(jnp.bfloat16)
    for n in range(TILES):
        cols = slice(n * tile, (n + 1) * tile)
        add = jnp.dot(hi, e[:, cols], preferred_element_type=jnp.float32)
        add += jnp.dot(mid, e[:, cols], preferred_element_type=jnp.float32)
        add += jnp.dot(low, e[:, cols], preferred_element_type=jnp.float32)
        acc[:, cols] = acc[:, cols] + adapter_scale * add

    per = block // SEGMENT_ROWS
    row = lax.broadcasted_iota(jnp.int32, (block, 1), 0)
    live = jnp.zeros((block, 1), jnp.int32)
    for i in range(per):
        live = jnp.where(row >= i * SEGMENT_ROWS, count_ref[z * per + i] + i * SEGMENT_ROWS, live)
    for i in range(1, steps):
        src = (z + i) % steps
        remote(
            q_recv.at[src], q_recv.at[src], q_send_sem.at[src], q_recv_sem.at[src], p, z
        ).wait_recv()
        remote(
            s_recv.at[src], s_recv.at[src], s_send_sem.at[src], s_recv_sem.at[src], p, z
        ).wait_recv()
    for n in range(TILES):
        cols = slice(n * tile, (n + 1) * tile)
        x = acc[:, cols]
        for i in range(1, steps):
            src = (z + i) % steps
            scale = s_recv[src].astype(jnp.float32)[:, n:n + 1]
            x = x + q_recv[src, :, cols].astype(jnp.int32).astype(jnp.float32) * scale
        out_ref[:, cols] = jnp.where(row < live, x, 0.0).astype(jnp.bfloat16)

    core_copy(p).wait_send()
    for k in range(CHUNKS):
        y_copy(k, p).wait_send()
        fwd_copy(k, y_peer).wait_send()
    for i in range(1, steps):
        blk = (z + i) % steps
        remote(
            q_send.at[blk], q_recv.at[z], q_send_sem.at[blk], q_recv_sem.at[z], p, blk
        ).wait_send()
        remote(
            s_send.at[blk], s_recv.at[z], s_send_sem.at[blk], s_recv_sem.at[z], p, blk
        ).wait_send()
    for t in range(steps):
        for i in range(pools):
            @pl.when(jnp.logical_or(z != t, p != i))
            def _():
                remote(
                    r_send.at[t], r_recv.at[me], r_send_sem.at[t * pools + i], r_recv_sem.at[me],
                    i, t,
                ).wait_send()


def fused_device(
    hidden,
    down_matrix,
    adapter_shrink_weight,
    adapter_expand_weight,
    segment_adapter_id,
    adapter_storage_slot,
    segment_row_count,
):
    pools, steps = lax.axis_size("pool"), lax.axis_size("tensor")
    block, ff = hidden.shape
    width = down_matrix.shape[1]
    owned, rank, _ = adapter_shrink_weight.shape
    adapters = adapter_expand_weight.shape[0]
    a = adapter_shrink_weight.reshape(owned * rank, ff)
    e = adapter_expand_weight.reshape(adapters * rank, width)
    f32, bf16 = jnp.float32, jnp.bfloat16
    dma = pltpu.SemaphoreType.DMA
    smem = pl.BlockSpec(memory_space=pltpu.SMEM)
    hbm = pl.BlockSpec(memory_space=pl.ANY)
    return pl.pallas_call(
        fused_kernel,
        out_shape=jax.ShapeDtypeStruct((block, width), bf16),
        in_specs=[smem] * 3 + [hbm] * 4,
        out_specs=pl.BlockSpec(memory_space=pltpu.VMEM),
        scratch_shapes=[
            pltpu.VMEM((pools, block, ff), bf16),
            pltpu.VMEM((TILES, ff, width // TILES), bf16),
            pltpu.VMEM((owned * rank, ff), bf16),
            pltpu.VMEM((adapters * rank, width), bf16),
            pltpu.VMEM((block, width), f32),
            pltpu.VMEM((steps, block, width), jnp.int16),
            pltpu.VMEM((steps, block, width), jnp.int16),
            pltpu.VMEM((steps, block, 128), bf16),
            pltpu.VMEM((steps, block, 128), bf16),
            pltpu.VMEM((steps, rank, block), f32),
            pltpu.VMEM((pools * steps, rank, block), f32),
            dma((TILES,)), dma((3,)), dma((CHUNKS,)), dma((CHUNKS,)), dma((1,)), dma((1,)),
            dma((CHUNKS,)), dma((CHUNKS,)), dma((steps,)), dma((steps,)), dma((steps,)),
            dma((steps,)), dma((pools * steps,)), dma((pools * steps,)),
        ],
        compiler_params=pltpu.CompilerParams(
            collective_id=0, has_side_effects=True, vmem_limit_bytes=VMEM_LIMIT
        ),
        cost_estimate=pl.CostEstimate(
            flops=2 * pools * block * ff * width, bytes_accessed=2 * ff * width, transcendentals=0
        ),
    )(segment_adapter_id, adapter_storage_slot, segment_row_count, hidden, down_matrix, a, e)


def fits(mesh, shapes):
    hidden, down = shapes
    parts = mesh.shape["groups"] * mesh.shape["pool"]
    rows = hidden[0] // parts
    ff, width = down[0] // mesh.shape["tensor"], down[1] // mesh.shape["pool"]
    return (
        mesh.shape["pool"] == 4
        and mesh.shape["tensor"] == 4
        and rows == 128
        and width % (128 * TILES) == 0
        and ff % 128 == 0
        and 2 * ff * (width + 4 * rows) < 40 * 2**20
    )


def solution(mesh):
    in_specs = (
        P(("groups", "pool"), "tensor"),
        P("tensor", "pool"),
        P("pool", None, "tensor"),
        P(None, None, "pool"),
        P("groups"),
        P(),
        P("groups"),
    )
    out_specs = P(("groups", "tensor"), "pool")

    def run(*args):
        body = fused_device if fits(mesh, (args[0].shape, args[1].shape)) else per_device
        return jax.shard_map(
            body, mesh=mesh, in_specs=in_specs, out_specs=out_specs, check_vma=False
        )(*args)

    return run
```

```python
import jax
import jax.numpy as jnp
from jax import lax
from jax.experimental import pallas as pl
from jax.experimental.pallas import tpu as pltpu
from jax.sharding import PartitionSpec as P

SEGMENT_ROWS = 16


adapter_scale = 2.0


def per_device(
    hidden,
    down_matrix,
    adapter_shrink_weight,
    adapter_expand_weight,
    segment_adapter_id,
    adapter_storage_slot,
    segment_row_count,
):
    gathered = lax.all_gather(hidden, "pool", axis=0, tiled=True)
    total_rows, ff_local = gathered.shape
    segments = total_rows // SEGMENT_ROWS
    base_output = jnp.dot(gathered, down_matrix, preferred_element_type=jnp.float32)
    adapter_ids = adapter_expand_weight.shape[0]
    same_id = segment_adapter_id[:, None] == jnp.arange(adapter_ids, dtype=jnp.int32)[None, :]
    storage_slot_index = jnp.sum(jnp.where(same_id, adapter_storage_slot[None, :], 0), axis=1)
    h_seg = gathered.reshape(segments, SEGMENT_ROWS, ff_local)
    every_adapter_id = lax.all_gather(adapter_shrink_weight, "pool", axis=0, tiled=True)
    chosen = jnp.take(every_adapter_id, storage_slot_index, axis=0)
    shrink = jnp.einsum("sgf,sqf->sgq", h_seg, chosen, preferred_element_type=jnp.float32)
    local_row_block = lax.psum_scatter(base_output, "tensor", scatter_dimension=0, tiled=True)
    local_segment_list = segments // lax.axis_size("tensor")
    first_seg = lax.axis_index("tensor") * local_segment_list
    whole_shrink = lax.psum(shrink, "tensor")
    own_shrink = lax.dynamic_slice_in_dim(whole_shrink, first_seg, local_segment_list, 0)
    owned_storage_slots = lax.dynamic_slice_in_dim(
        storage_slot_index, first_seg, local_segment_list, 0
    )
    owned_expand_weight = jnp.take(adapter_expand_weight, owned_storage_slots, axis=0).astype(
        jnp.float32
    )
    expand_output = jnp.einsum(
        "sgq,sqd->sgd", own_shrink, owned_expand_weight, precision=lax.Precision.HIGHEST
    )
    local_row_block = local_row_block + adapter_scale * expand_output.reshape(
        local_segment_list * SEGMENT_ROWS, -1
    )
    counts = lax.dynamic_slice_in_dim(segment_row_count, first_seg, local_segment_list, 0)
    valid_mask = (jnp.arange(SEGMENT_ROWS, dtype=jnp.int32)[None, :] < counts[:, None]).reshape(-1)
    return jnp.where(valid_mask[:, None], local_row_block, 0.0).astype(jnp.bfloat16)


MESH = pl.DeviceIdType.MESH
LEVELS = 32500.0
TILES = 4
VMEM_LIMIT = 60 * 2**20
PIECES = 8
NEAR = (4, 4)
FAR = (2, 3, 2, 1)


def fused_kernel(
    id_ref, slot_ref, count_ref, hidden_ref, down_ref, shrink_ref, expand_ref, out_ref,
    h, w, a, e, acc, stash, q_send, q_recv, s_send, s_recv, m_recv, ms_recv, r_send, r_recv,
    w_sem, load_sem, y_send_sem, y_recv_sem, c_send_sem, c_recv_sem, f_send_sem, f_recv_sem,
    q_send_sem, q_recv_sem, s_send_sem, s_recv_sem, m_recv_sem, ms_recv_sem, r_send_sem, r_recv_sem,
):
    pools, steps = lax.axis_size("pool"), lax.axis_size("tensor")
    g, p, z = lax.axis_index("groups"), lax.axis_index("pool"), lax.axis_index("tensor")
    y, c = p // 2, p % 2
    core_peer = y * 2 + (1 - c)
    y_peer = (1 - y) * 2 + c
    block, ff = h.shape[1], h.shape[2]
    tile = w.shape[2]
    part = block // PIECES
    rank = r_send.shape[1]
    owned = a.shape[0] // rank

    def remote(src, dst, send, recv, pool, step):
        return pltpu.make_async_remote_copy(
            src_ref=src, dst_ref=dst, send_sem=send, recv_sem=recv,
            device_id=(g, pool, step), device_id_type=MESH,
        )

    def w_copy(n):
        return pltpu.make_async_copy(
            down_ref.at[:, pl.ds(pl.multiple_of(n * tile, tile), tile)], w.at[n], w_sem.at[n]
        )

    own_load = pltpu.make_async_copy(hidden_ref, h.at[p], load_sem.at[0])
    a_load = pltpu.make_async_copy(shrink_ref, a, load_sem.at[1])
    e_load = pltpu.make_async_copy(expand_ref, e, load_sem.at[2])
    own_load.start()
    for n in range(TILES):
        w_copy(n).start()

    barrier = pltpu.get_barrier_semaphore()
    for i in range(1, pools * steps):
        other = (p * steps + z + i) % (pools * steps)
        pl.semaphore_signal(
            barrier, inc=1, device_id=(g, other // steps, other % steps), device_id_type=MESH
        )
    pl.semaphore_wait(barrier, pools * steps - 1)

    def y_copy(k, blk):
        rows = pl.ds(pl.multiple_of(k * part, part), part)
        return remote(
            hidden_ref.at[rows], h.at[blk, rows], y_send_sem.at[k], y_recv_sem.at[k], y_peer, z
        )

    def fwd_copy(k, blk):
        rows = pl.ds(pl.multiple_of(k * part, part), part)
        return remote(
            h.at[blk, rows], h.at[blk, rows], f_send_sem.at[k], f_recv_sem.at[k], core_peer, z
        )

    def core_copy(blk):
        return remote(hidden_ref, h.at[blk], c_send_sem.at[0], c_recv_sem.at[0], core_peer, z)

    y_copy(0, p).start()
    core_copy(p).start()
    for k in range(1, PIECES):
        y_copy(k, p).start()
    a_load.start()
    e_load.start()

    def inner(half):
        return 2 - half

    def code(x, n, scales):
        top = jnp.max(jnp.abs(x), axis=1, keepdims=True)
        scale = (jnp.maximum(top, 1e-30) * (1.0 / LEVELS)).astype(jnp.bfloat16).astype(jnp.float32)
        coded = jnp.round(x * (1.0 / scale)).astype(jnp.int32).astype(jnp.int16)
        lane = lax.broadcasted_iota(jnp.int32, scales.shape, 1)
        return coded, jnp.where(lane == n, scale, scales)

    def decode(coded, slab, n):
        return coded.astype(jnp.int32).astype(jnp.float32) * slab.astype(jnp.float32)[:, n:n + 1]

    def post(blk, half, j, u, here, cols, scale_send):
        q, ready, to_own, own_sem, to_inner, inner_sem = (
            (s_send, s_send_sem, s_recv, s_recv_sem, ms_recv, ms_recv_sem)
            if scale_send
            else (q_send, q_send_sem, q_recv, q_recv_sem, m_recv, m_recv_sem)
        )

        @pl.when(z // 2 == half)
        def _():
            remote(
                q.at[blk, here, cols], to_own.at[0, here, cols],
                ready.at[blk], own_sem.at[0], p, blk,
            ).start()

        @pl.when(z // 2 != half)
        def _():
            remote(
                q.at[blk, here, cols], to_inner.at[j, here, cols],
                ready.at[blk], inner_sem.at[u], p, inner(half),
            ).start()

    lanes = pl.ds(0, 128)

    def unit(half, first, rows, u, loads):
        here = pl.ds(first, rows)

        def body(n, scales):
            if loads:
                w_copy(n).wait()
            lhs = jnp.concatenate([h[2 * half, here], h[2 * half + 1, here]], axis=0)
            x = jnp.dot(lhs, w[n], preferred_element_type=jnp.float32)
            cols = pl.ds(pl.multiple_of(n * tile, tile), tile)
            out = []
            for j in range(2):
                blk = 2 * half + j
                xj = x[j * rows:(j + 1) * rows]
                coded, sc = code(xj, n, scales[j])
                out.append(sc)

                @pl.when(blk == z)
                def _():
                    acc[here, cols] = xj

                @pl.when(z == inner(half))
                def _():
                    stash[j, here, cols] = xj

                @pl.when(jnp.logical_and(blk != z, z != inner(half)))
                def _():
                    q_send[blk, here, cols] = coded
                    post(blk, half, j, u, here, cols, False)
            return tuple(out)

        zero = jnp.zeros((rows, 128), jnp.float32)
        scales = lax.fori_loop(0, TILES, body, (zero, zero))
        for j in range(2):
            blk = 2 * half + j

            @pl.when(jnp.logical_and(blk != z, z != inner(half)))
            def _():
                s_send[blk, here] = scales[j].astype(jnp.bfloat16)
                post(blk, half, j, u, here, lanes, True)

    def merge(half, first, rows, u):
        here = pl.ds(first, rows)

        @pl.when(z == inner(half))
        def _():
            remote(
                m_recv.at[:, here], m_recv.at[:, here], q_send_sem.at[0], m_recv_sem.at[u], p, z
            ).wait_recv()
            remote(
                ms_recv.at[:, here], ms_recv.at[:, here], s_send_sem.at[0], ms_recv_sem.at[u], p, z
            ).wait_recv()
            scales = [jnp.zeros((rows, 128), jnp.float32)] * 2
            for n in range(TILES):
                cols = pl.ds(n * tile, tile)
                for j in range(2):
                    blk = 2 * half + j
                    x = stash[j, here, cols] + decode(m_recv[j, here, cols], ms_recv[j, here], n)
                    coded, scales[j] = code(x, n, scales[j])
                    q_send[blk, here, cols] = coded
                    remote(
                        q_send.at[blk, here, cols], q_recv.at[1, here, cols],
                        q_send_sem.at[blk], q_recv_sem.at[1], p, blk,
                    ).start()
            for j in range(2):
                blk = 2 * half + j
                s_send[blk, here] = scales[j].astype(jnp.bfloat16)
                remote(
                    s_send.at[blk, here], s_recv.at[1, here],
                    s_send_sem.at[blk], s_recv_sem.at[1], p, blk,
                ).start()

    def slots_of(blk):
        per = block // SEGMENT_ROWS
        lane = lax.broadcasted_iota(jnp.int32, (1, block), 1)
        vec = jnp.zeros((1, block), jnp.int32)
        for i in range(per):
            vec = jnp.where(lane >= i * SEGMENT_ROWS, slot_ref[id_ref[blk * per + i]], vec)
        return vec

    def shrink_block(blk):
        s = lax.dot_general(
            a[...], h[blk], (((1,), (1,)), ((), ())), preferred_element_type=jnp.float32
        )
        row_slot = lax.broadcasted_iota(jnp.int32, s.shape, 0) // rank + owned * p
        s = jnp.where(row_slot == slots_of(blk), s, 0.0)
        total = s[0:rank]
        for i in range(1, owned):
            total = total + s[i * rank:(i + 1) * rank]
        r_send[blk] = total
        me = p * steps + z

        @pl.when(blk == z)
        def _():
            r_recv[me] = total

        for i in range(pools):
            @pl.when(jnp.logical_or(blk != z, p != i))
            def _():
                remote(
                    r_send.at[blk], r_recv.at[me],
                    r_send_sem.at[blk * pools + i], r_recv_sem.at[me], i, blk,
                ).start()

    own_load.wait()
    remote(
        hidden_ref, h.at[core_peer], c_send_sem.at[0], c_recv_sem.at[0], core_peer, z
    ).wait_recv()

    near, far = [], []
    for sizes, units in ((NEAR, near), (FAR, far)):
        start = 0
        for size in sizes:
            units.append((start * part, size * part))
            start += size

    def near_merge(i):
        merge(y, *near[i], i)

    def far_merge(i):
        merge(1 - y, *far[i], len(near) + i)

    for i, rows in enumerate(near):
        unit(y, *rows, i, i == 0)
    a_load.wait()

    def near_shrink(j, _):
        shrink_block(y * 2 + j)
        return 0

    lax.fori_loop(0, 2, near_shrink, 0)

    for i, (first, rows) in enumerate(far):
        pieces = range(first // part, (first + rows) // part)
        for k in pieces:
            y_copy(k, y_peer).wait_recv()
            fwd_copy(k, y_peer).start()
        for k in pieces:
            fwd_copy(k, (1 - y) * 2 + (1 - c)).wait_recv()
        unit(1 - y, first, rows, len(near) + i, False)
        if i < len(near):
            near_merge(i)
        if i >= 1:
            far_merge(i - 1)

    def far_shrink(j, _):
        shrink_block((1 - y) * 2 + j)
        return 0

    lax.fori_loop(0, 2, far_shrink, 0)
    far_merge(len(far) - 1)

    me = p * steps + z
    e_load.wait()
    for i in range(pools * steps):
        @pl.when(me != i)
        def _():
            remote(
                r_recv.at[i], r_recv.at[i], r_send_sem.at[i], r_recv_sem.at[i], p, z
            ).wait_recv()
    whole = r_recv[0]
    for i in range(1, pools * steps):
        whole = whole + r_recv[i]
    adapters = e.shape[0] // rank
    spread = jnp.concatenate([whole] * adapters, axis=0)
    row_slot = lax.broadcasted_iota(jnp.int32, spread.shape, 0) // rank
    spread = jnp.where(row_slot == slots_of(z), spread, 0.0).T
    hi = spread.astype(jnp.bfloat16)
    rest = spread - hi.astype(jnp.float32)
    mid = rest.astype(jnp.bfloat16)
    low = (rest - mid.astype(jnp.float32)).astype(jnp.bfloat16)
    for n in range(TILES):
        cols = slice(n * tile, (n + 1) * tile)
        add = jnp.dot(hi, e[:, cols], preferred_element_type=jnp.float32)
        add += jnp.dot(mid, e[:, cols], preferred_element_type=jnp.float32)
        add += jnp.dot(low, e[:, cols], preferred_element_type=jnp.float32)
        acc[:, cols] = acc[:, cols] + adapter_scale * add

    per = block // SEGMENT_ROWS
    row = lax.broadcasted_iota(jnp.int32, (block, 1), 0)
    live = jnp.zeros((block, 1), jnp.int32)
    for i in range(per):
        live = jnp.where(row >= i * SEGMENT_ROWS, count_ref[z * per + i] + i * SEGMENT_ROWS, live)
    for src in range(2):
        remote(
            q_recv.at[src], q_recv.at[src], q_send_sem.at[src], q_recv_sem.at[src], p, z
        ).wait_recv()
        remote(
            s_recv.at[src], s_recv.at[src], s_send_sem.at[src], s_recv_sem.at[src], p, z
        ).wait_recv()
    for n in range(TILES):
        cols = slice(n * tile, (n + 1) * tile)
        x = acc[:, cols]
        for src in range(2):
            x = x + decode(q_recv[src, :, cols], s_recv[src], n)
        out_ref[:, cols] = jnp.where(row < live, x, 0.0).astype(jnp.bfloat16)

    core_copy(p).wait_send()
    for k in range(PIECES):
        y_copy(k, p).wait_send()
        fwd_copy(k, y_peer).wait_send()
    for i in range(1, steps):
        blk = (z + i) % steps
        remote(
            q_send.at[blk], q_recv.at[0], q_send_sem.at[blk], q_recv_sem.at[0], p, blk
        ).wait_send()
        remote(
            s_send.at[blk], s_recv.at[0], s_send_sem.at[blk], s_recv_sem.at[0], p, blk
        ).wait_send()
    for t in range(steps):
        for i in range(pools):
            @pl.when(jnp.logical_or(z != t, p != i))
            def _():
                remote(
                    r_send.at[t], r_recv.at[me], r_send_sem.at[t * pools + i], r_recv_sem.at[me],
                    i, t,
                ).wait_send()


def fused_device(
    hidden,
    down_matrix,
    adapter_shrink_weight,
    adapter_expand_weight,
    segment_adapter_id,
    adapter_storage_slot,
    segment_row_count,
):
    pools, steps = lax.axis_size("pool"), lax.axis_size("tensor")
    block, ff = hidden.shape
    width = down_matrix.shape[1]
    owned, rank, _ = adapter_shrink_weight.shape
    adapters = adapter_expand_weight.shape[0]
    a = adapter_shrink_weight.reshape(owned * rank, ff)
    e = adapter_expand_weight.reshape(adapters * rank, width)
    f32, bf16 = jnp.float32, jnp.bfloat16
    dma = pltpu.SemaphoreType.DMA
    smem = pl.BlockSpec(memory_space=pltpu.SMEM)
    hbm = pl.BlockSpec(memory_space=pl.ANY)
    return pl.pallas_call(
        fused_kernel,
        out_shape=jax.ShapeDtypeStruct((block, width), bf16),
        in_specs=[smem] * 3 + [hbm] * 4,
        out_specs=pl.BlockSpec(memory_space=pltpu.VMEM),
        scratch_shapes=[
            pltpu.VMEM((pools, block, ff), bf16),
            pltpu.VMEM((TILES, ff, width // TILES), bf16),
            pltpu.VMEM((owned * rank, ff), bf16),
            pltpu.VMEM((adapters * rank, width), bf16),
            pltpu.VMEM((block, width), f32),
            pltpu.VMEM((2, block, width), f32),
            pltpu.VMEM((steps, block, width), jnp.int16),
            pltpu.VMEM((2, block, width), jnp.int16),
            pltpu.VMEM((steps, block, 128), bf16),
            pltpu.VMEM((2, block, 128), bf16),
            pltpu.VMEM((2, block, width), jnp.int16),
            pltpu.VMEM((2, block, 128), bf16),
            pltpu.VMEM((steps, rank, block), f32),
            pltpu.VMEM((pools * steps, rank, block), f32),
            dma((TILES,)), dma((3,)), dma((PIECES,)), dma((PIECES,)), dma((1,)), dma((1,)),
            dma((PIECES,)), dma((PIECES,)), dma((steps,)), dma((2,)), dma((steps,)), dma((2,)),
            dma((len(NEAR + FAR),)), dma((len(NEAR + FAR),)), dma((pools * steps,)), dma((pools * steps,)),
        ],
        compiler_params=pltpu.CompilerParams(
            collective_id=0, has_side_effects=True, vmem_limit_bytes=VMEM_LIMIT
        ),
        cost_estimate=pl.CostEstimate(
            flops=2 * pools * block * ff * width, bytes_accessed=2 * ff * width, transcendentals=0
        ),
    )(segment_adapter_id, adapter_storage_slot, segment_row_count, hidden, down_matrix, a, e)


def fits(mesh, shapes):
    hidden, down = shapes
    parts = mesh.shape["groups"] * mesh.shape["pool"]
    rows = hidden[0] // parts
    ff, width = down[0] // mesh.shape["tensor"], down[1] // mesh.shape["pool"]
    return (
        mesh.shape["pool"] == 4
        and mesh.shape["tensor"] == 4
        and rows == 128
        and width % (128 * TILES) == 0
        and ff % 128 == 0
        and 2 * ff * (width + 4 * rows) < 40 * 2**20
    )


def solution(mesh):
    in_specs = (
        P(("groups", "pool"), "tensor"),
        P("tensor", "pool"),
        P("pool", None, "tensor"),
        P(None, None, "pool"),
        P("groups"),
        P(),
        P("groups"),
    )
    out_specs = P(("groups", "tensor"), "pool")

    def run(*args):
        body = fused_device if fits(mesh, (args[0].shape, args[1].shape)) else per_device
        return jax.shard_map(
            body, mesh=mesh, in_specs=in_specs, out_specs=out_specs, check_vma=False
        )(*args)

    return run
```

```python
import jax
import jax.numpy as jnp
from jax import lax
from jax.experimental import pallas as pl
from jax.experimental.pallas import tpu as pltpu
from jax.sharding import PartitionSpec as P

SEGMENT_ROWS = 16


adapter_scale = 2.0


def per_device(
    hidden,
    down_matrix,
    adapter_shrink_weight,
    adapter_expand_weight,
    segment_adapter_id,
    adapter_storage_slot,
    segment_row_count,
):
    gathered = lax.all_gather(hidden, "pool", axis=0, tiled=True)
    total_rows, ff_local = gathered.shape
    segments = total_rows // SEGMENT_ROWS
    base_output = jnp.dot(gathered, down_matrix, preferred_element_type=jnp.float32)
    adapter_ids = adapter_expand_weight.shape[0]
    same_id = segment_adapter_id[:, None] == jnp.arange(adapter_ids, dtype=jnp.int32)[None, :]
    storage_slot_index = jnp.sum(jnp.where(same_id, adapter_storage_slot[None, :], 0), axis=1)
    h_seg = gathered.reshape(segments, SEGMENT_ROWS, ff_local)
    every_adapter_id = lax.all_gather(adapter_shrink_weight, "pool", axis=0, tiled=True)
    chosen = jnp.take(every_adapter_id, storage_slot_index, axis=0)
    shrink = jnp.einsum("sgf,sqf->sgq", h_seg, chosen, preferred_element_type=jnp.float32)
    local_row_block = lax.psum_scatter(base_output, "tensor", scatter_dimension=0, tiled=True)
    local_segment_list = segments // lax.axis_size("tensor")
    first_seg = lax.axis_index("tensor") * local_segment_list
    whole_shrink = lax.psum(shrink, "tensor")
    own_shrink = lax.dynamic_slice_in_dim(whole_shrink, first_seg, local_segment_list, 0)
    owned_storage_slots = lax.dynamic_slice_in_dim(
        storage_slot_index, first_seg, local_segment_list, 0
    )
    owned_expand_weight = jnp.take(adapter_expand_weight, owned_storage_slots, axis=0).astype(
        jnp.float32
    )
    expand_output = jnp.einsum(
        "sgq,sqd->sgd", own_shrink, owned_expand_weight, precision=lax.Precision.HIGHEST
    )
    local_row_block = local_row_block + adapter_scale * expand_output.reshape(
        local_segment_list * SEGMENT_ROWS, -1
    )
    counts = lax.dynamic_slice_in_dim(segment_row_count, first_seg, local_segment_list, 0)
    valid_mask = (jnp.arange(SEGMENT_ROWS, dtype=jnp.int32)[None, :] < counts[:, None]).reshape(-1)
    return jnp.where(valid_mask[:, None], local_row_block, 0.0).astype(jnp.bfloat16)


MESH = pl.DeviceIdType.MESH
LEVELS = 32500.0
TILES = 4
VMEM_LIMIT = 60 * 2**20
PIECES = 8
NEAR = (8,)
FAR = (2, 3, 2, 1)


def fused_kernel(
    id_ref, slot_ref, count_ref, hidden_ref, down_ref, shrink_ref, expand_ref, out_ref,
    h, w, a, e, acc, stash, q_send, q_recv, s_send, s_recv, m_recv, ms_recv, r_send, r_recv,
    w_sem, load_sem, y_send_sem, y_recv_sem, c_send_sem, c_recv_sem, f_send_sem, f_recv_sem,
    q_send_sem, q_recv_sem, s_send_sem, s_recv_sem, m_recv_sem, ms_recv_sem, r_send_sem, r_recv_sem,
):
    pools, steps = lax.axis_size("pool"), lax.axis_size("tensor")
    g, p, z = lax.axis_index("groups"), lax.axis_index("pool"), lax.axis_index("tensor")
    y, c = p // 2, p % 2
    core_peer = y * 2 + (1 - c)
    y_peer = (1 - y) * 2 + c
    block, ff = h.shape[1], h.shape[2]
    tile = w.shape[2]
    part = block // PIECES
    rank = r_send.shape[1]
    owned = a.shape[0] // rank

    def remote(src, dst, send, recv, pool, step):
        return pltpu.make_async_remote_copy(
            src_ref=src, dst_ref=dst, send_sem=send, recv_sem=recv,
            device_id=(g, pool, step), device_id_type=MESH,
        )

    def w_copy(n):
        return pltpu.make_async_copy(
            down_ref.at[:, pl.ds(pl.multiple_of(n * tile, tile), tile)], w.at[n], w_sem.at[n]
        )

    own_load = pltpu.make_async_copy(hidden_ref, h.at[p], load_sem.at[0])
    a_load = pltpu.make_async_copy(shrink_ref, a, load_sem.at[1])
    e_load = pltpu.make_async_copy(expand_ref, e, load_sem.at[2])
    own_load.start()
    for n in range(TILES):
        w_copy(n).start()

    barrier = pltpu.get_barrier_semaphore()
    for i in range(1, pools * steps):
        other = (p * steps + z + i) % (pools * steps)
        pl.semaphore_signal(
            barrier, inc=1, device_id=(g, other // steps, other % steps), device_id_type=MESH
        )
    pl.semaphore_wait(barrier, pools * steps - 1)

    def y_copy(k, blk):
        rows = pl.ds(pl.multiple_of(k * part, part), part)
        return remote(
            hidden_ref.at[rows], h.at[blk, rows], y_send_sem.at[k], y_recv_sem.at[k], y_peer, z
        )

    def fwd_copy(k, blk):
        rows = pl.ds(pl.multiple_of(k * part, part), part)
        return remote(
            h.at[blk, rows], h.at[blk, rows], f_send_sem.at[k], f_recv_sem.at[k], core_peer, z
        )

    def core_copy(blk):
        return remote(hidden_ref, h.at[blk], c_send_sem.at[0], c_recv_sem.at[0], core_peer, z)

    y_copy(0, p).start()
    core_copy(p).start()
    for k in range(1, PIECES):
        y_copy(k, p).start()
    a_load.start()
    e_load.start()

    def inner(half):
        return 2 - half

    def code(x, n, scales):
        top = jnp.max(jnp.abs(x), axis=1, keepdims=True)
        scale = (jnp.maximum(top, 1e-30) * (1.0 / LEVELS)).astype(jnp.bfloat16).astype(jnp.float32)
        coded = jnp.round(x * (1.0 / scale)).astype(jnp.int32).astype(jnp.int16)
        lane = lax.broadcasted_iota(jnp.int32, scales.shape, 1)
        return coded, jnp.where(lane == n, scale, scales)

    def decode(coded, slab, n):
        return coded.astype(jnp.int32).astype(jnp.float32) * slab.astype(jnp.float32)[:, n:n + 1]

    def post(blk, half, j, u, here, cols, scale_send):
        q, ready, to_own, own_sem, to_inner, inner_sem = (
            (s_send, s_send_sem, s_recv, s_recv_sem, ms_recv, ms_recv_sem)
            if scale_send
            else (q_send, q_send_sem, q_recv, q_recv_sem, m_recv, m_recv_sem)
        )

        @pl.when(z // 2 == half)
        def _():
            remote(
                q.at[blk, here, cols], to_own.at[0, here, cols],
                ready.at[blk], own_sem.at[0], p, blk,
            ).start()

        @pl.when(z // 2 != half)
        def _():
            remote(
                q.at[blk, here, cols], to_inner.at[j, here, cols],
                ready.at[blk], inner_sem.at[u], p, inner(half),
            ).start()

    lanes = pl.ds(0, 128)

    def unit(half, first, rows, u, loads):
        here = pl.ds(first, rows)

        def body(n, scales):
            if loads:
                w_copy(n).wait()
            lhs = jnp.concatenate([h[2 * half, here], h[2 * half + 1, here]], axis=0)
            x = jnp.dot(lhs, w[n], preferred_element_type=jnp.float32)
            cols = pl.ds(pl.multiple_of(n * tile, tile), tile)
            out = []
            for j in range(2):
                blk = 2 * half + j
                xj = x[j * rows:(j + 1) * rows]
                coded, sc = code(xj, n, scales[j])
                out.append(sc)

                @pl.when(blk == z)
                def _():
                    acc[here, cols] = xj

                @pl.when(z == inner(half))
                def _():
                    stash[j, here, cols] = xj

                @pl.when(jnp.logical_and(blk != z, z != inner(half)))
                def _():
                    q_send[blk, here, cols] = coded
                    post(blk, half, j, u, here, cols, False)
            return tuple(out)

        zero = jnp.zeros((rows, 128), jnp.float32)
        scales = lax.fori_loop(0, TILES, body, (zero, zero))
        for j in range(2):
            blk = 2 * half + j

            @pl.when(jnp.logical_and(blk != z, z != inner(half)))
            def _():
                s_send[blk, here] = scales[j].astype(jnp.bfloat16)
                post(blk, half, j, u, here, lanes, True)

    def merge(half, first, rows, u):
        here = pl.ds(first, rows)

        @pl.when(z == inner(half))
        def _():
            remote(
                m_recv.at[:, here], m_recv.at[:, here], q_send_sem.at[0], m_recv_sem.at[u], p, z
            ).wait_recv()
            remote(
                ms_recv.at[:, here], ms_recv.at[:, here], s_send_sem.at[0], ms_recv_sem.at[u], p, z
            ).wait_recv()
            scales = [jnp.zeros((rows, 128), jnp.float32)] * 2
            for n in range(TILES):
                cols = pl.ds(n * tile, tile)
                for j in range(2):
                    blk = 2 * half + j
                    x = stash[j, here, cols] + decode(m_recv[j, here, cols], ms_recv[j, here], n)
                    coded, scales[j] = code(x, n, scales[j])
                    q_send[blk, here, cols] = coded
                    remote(
                        q_send.at[blk, here, cols], q_recv.at[1, here, cols],
                        q_send_sem.at[blk], q_recv_sem.at[1], p, blk,
                    ).start()
            for j in range(2):
                blk = 2 * half + j
                s_send[blk, here] = scales[j].astype(jnp.bfloat16)
                remote(
                    s_send.at[blk, here], s_recv.at[1, here],
                    s_send_sem.at[blk], s_recv_sem.at[1], p, blk,
                ).start()

    def slots_of(blk):
        per = block // SEGMENT_ROWS
        lane = lax.broadcasted_iota(jnp.int32, (1, block), 1)
        vec = jnp.zeros((1, block), jnp.int32)
        for i in range(per):
            vec = jnp.where(lane >= i * SEGMENT_ROWS, slot_ref[id_ref[blk * per + i]], vec)
        return vec

    def shrink_block(blk):
        s = lax.dot_general(
            a[...], h[blk], (((1,), (1,)), ((), ())), preferred_element_type=jnp.float32
        )
        row_slot = lax.broadcasted_iota(jnp.int32, s.shape, 0) // rank + owned * p
        s = jnp.where(row_slot == slots_of(blk), s, 0.0)
        total = s[0:rank]
        for i in range(1, owned):
            total = total + s[i * rank:(i + 1) * rank]
        r_send[blk] = total
        me = p * steps + z

        @pl.when(blk == z)
        def _():
            r_recv[me] = total

        for i in range(pools):
            @pl.when(jnp.logical_or(blk != z, p != i))
            def _():
                remote(
                    r_send.at[blk], r_recv.at[me],
                    r_send_sem.at[blk * pools + i], r_recv_sem.at[me], i, blk,
                ).start()

    own_load.wait()
    remote(
        hidden_ref, h.at[core_peer], c_send_sem.at[0], c_recv_sem.at[0], core_peer, z
    ).wait_recv()

    near, far = [], []
    for sizes, units in ((NEAR, near), (FAR, far)):
        start = 0
        for size in sizes:
            units.append((start * part, size * part))
            start += size

    def near_merge(i):
        merge(y, *near[i], i)

    def far_merge(i):
        merge(1 - y, *far[i], len(near) + i)

    for i, rows in enumerate(near):
        unit(y, *rows, i, i == 0)
    a_load.wait()

    def near_shrink(j, _):
        shrink_block(y * 2 + j)
        return 0

    lax.fori_loop(0, 2, near_shrink, 0)

    for i, (first, rows) in enumerate(far):
        pieces = range(first // part, (first + rows) // part)
        for k in pieces:
            y_copy(k, y_peer).wait_recv()
            fwd_copy(k, y_peer).start()
        for k in pieces:
            fwd_copy(k, (1 - y) * 2 + (1 - c)).wait_recv()
        unit(1 - y, first, rows, len(near) + i, False)
        if i < len(near):
            near_merge(i)
        if i >= 1:
            far_merge(i - 1)

    def far_shrink(j, _):
        shrink_block((1 - y) * 2 + j)
        return 0

    lax.fori_loop(0, 2, far_shrink, 0)
    far_merge(len(far) - 1)

    me = p * steps + z
    e_load.wait()
    for i in range(pools * steps):
        @pl.when(me != i)
        def _():
            remote(
                r_recv.at[i], r_recv.at[i], r_send_sem.at[i], r_recv_sem.at[i], p, z
            ).wait_recv()
    whole = r_recv[0]
    for i in range(1, pools * steps):
        whole = whole + r_recv[i]
    adapters = e.shape[0] // rank
    spread = jnp.concatenate([whole] * adapters, axis=0)
    row_slot = lax.broadcasted_iota(jnp.int32, spread.shape, 0) // rank
    spread = jnp.where(row_slot == slots_of(z), spread, 0.0).T
    hi = spread.astype(jnp.bfloat16)
    rest = spread - hi.astype(jnp.float32)
    mid = rest.astype(jnp.bfloat16)
    low = (rest - mid.astype(jnp.float32)).astype(jnp.bfloat16)
    for n in range(TILES):
        cols = slice(n * tile, (n + 1) * tile)
        add = jnp.dot(hi, e[:, cols], preferred_element_type=jnp.float32)
        add += jnp.dot(mid, e[:, cols], preferred_element_type=jnp.float32)
        add += jnp.dot(low, e[:, cols], preferred_element_type=jnp.float32)
        acc[:, cols] = acc[:, cols] + adapter_scale * add

    per = block // SEGMENT_ROWS
    row = lax.broadcasted_iota(jnp.int32, (block, 1), 0)
    live = jnp.zeros((block, 1), jnp.int32)
    for i in range(per):
        live = jnp.where(row >= i * SEGMENT_ROWS, count_ref[z * per + i] + i * SEGMENT_ROWS, live)
    for src in range(2):
        remote(
            q_recv.at[src], q_recv.at[src], q_send_sem.at[src], q_recv_sem.at[src], p, z
        ).wait_recv()
        remote(
            s_recv.at[src], s_recv.at[src], s_send_sem.at[src], s_recv_sem.at[src], p, z
        ).wait_recv()
    for n in range(TILES):
        cols = slice(n * tile, (n + 1) * tile)
        x = acc[:, cols]
        for src in range(2):
            x = x + decode(q_recv[src, :, cols], s_recv[src], n)
        out_ref[:, cols] = jnp.where(row < live, x, 0.0).astype(jnp.bfloat16)

    core_copy(p).wait_send()
    for k in range(PIECES):
        y_copy(k, p).wait_send()
        fwd_copy(k, y_peer).wait_send()
    for i in range(1, steps):
        blk = (z + i) % steps
        remote(
            q_send.at[blk], q_recv.at[0], q_send_sem.at[blk], q_recv_sem.at[0], p, blk
        ).wait_send()
        remote(
            s_send.at[blk], s_recv.at[0], s_send_sem.at[blk], s_recv_sem.at[0], p, blk
        ).wait_send()
    for t in range(steps):
        for i in range(pools):
            @pl.when(jnp.logical_or(z != t, p != i))
            def _():
                remote(
                    r_send.at[t], r_recv.at[me], r_send_sem.at[t * pools + i], r_recv_sem.at[me],
                    i, t,
                ).wait_send()


def fused_device(
    hidden,
    down_matrix,
    adapter_shrink_weight,
    adapter_expand_weight,
    segment_adapter_id,
    adapter_storage_slot,
    segment_row_count,
):
    pools, steps = lax.axis_size("pool"), lax.axis_size("tensor")
    block, ff = hidden.shape
    width = down_matrix.shape[1]
    owned, rank, _ = adapter_shrink_weight.shape
    adapters = adapter_expand_weight.shape[0]
    a = adapter_shrink_weight.reshape(owned * rank, ff)
    e = adapter_expand_weight.reshape(adapters * rank, width)
    f32, bf16 = jnp.float32, jnp.bfloat16
    dma = pltpu.SemaphoreType.DMA
    smem = pl.BlockSpec(memory_space=pltpu.SMEM)
    hbm = pl.BlockSpec(memory_space=pl.ANY)
    return pl.pallas_call(
        fused_kernel,
        out_shape=jax.ShapeDtypeStruct((block, width), bf16),
        in_specs=[smem] * 3 + [hbm] * 4,
        out_specs=pl.BlockSpec(memory_space=pltpu.VMEM),
        scratch_shapes=[
            pltpu.VMEM((pools, block, ff), bf16),
            pltpu.VMEM((TILES, ff, width // TILES), bf16),
            pltpu.VMEM((owned * rank, ff), bf16),
            pltpu.VMEM((adapters * rank, width), bf16),
            pltpu.VMEM((block, width), f32),
            pltpu.VMEM((2, block, width), f32),
            pltpu.VMEM((steps, block, width), jnp.int16),
            pltpu.VMEM((2, block, width), jnp.int16),
            pltpu.VMEM((steps, block, 128), bf16),
            pltpu.VMEM((2, block, 128), bf16),
            pltpu.VMEM((2, block, width), jnp.int16),
            pltpu.VMEM((2, block, 128), bf16),
            pltpu.VMEM((steps, rank, block), f32),
            pltpu.VMEM((pools * steps, rank, block), f32),
            dma((TILES,)), dma((3,)), dma((PIECES,)), dma((PIECES,)), dma((1,)), dma((1,)),
            dma((PIECES,)), dma((PIECES,)), dma((steps,)), dma((2,)), dma((steps,)), dma((2,)),
            dma((len(NEAR + FAR),)), dma((len(NEAR + FAR),)), dma((pools * steps,)), dma((pools * steps,)),
        ],
        compiler_params=pltpu.CompilerParams(
            collective_id=0, has_side_effects=True, vmem_limit_bytes=VMEM_LIMIT
        ),
        cost_estimate=pl.CostEstimate(
            flops=2 * pools * block * ff * width, bytes_accessed=2 * ff * width, transcendentals=0
        ),
    )(segment_adapter_id, adapter_storage_slot, segment_row_count, hidden, down_matrix, a, e)


def fits(mesh, shapes):
    hidden, down = shapes
    parts = mesh.shape["groups"] * mesh.shape["pool"]
    rows = hidden[0] // parts
    ff, width = down[0] // mesh.shape["tensor"], down[1] // mesh.shape["pool"]
    return (
        mesh.shape["pool"] == 4
        and mesh.shape["tensor"] == 4
        and rows == 128
        and width % (128 * TILES) == 0
        and ff % 128 == 0
        and 2 * ff * (width + 4 * rows) < 40 * 2**20
    )


def solution(mesh):
    in_specs = (
        P(("groups", "pool"), "tensor"),
        P("tensor", "pool"),
        P("pool", None, "tensor"),
        P(None, None, "pool"),
        P("groups"),
        P(),
        P("groups"),
    )
    out_specs = P(("groups", "tensor"), "pool")

    def run(*args):
        body = fused_device if fits(mesh, (args[0].shape, args[1].shape)) else per_device
        return jax.shard_map(
            body, mesh=mesh, in_specs=in_specs, out_specs=out_specs, check_vma=False
        )(*args)

    return run
```
